32 devices in a mesh: ens: 8 (over y, x, core), lat: 4 (over z).
Axes of the slice: x: 2, y: 2, z: 4, core: 2. Of those that a mesh axis runs over, the one named last changes fastest.
Arguments:
- ensemble: float32 [32, 3, 2, 256, 1440], P('ens', None, None, 'lat'), may hold values from -6 to 6
- ancestors: int32 [32], P('ens'), may hold values from 0 to 31, as said below
- depth: float32 [2, 256, 1440], P(None, 'lat'), may hold values from 0.3 to 1
- forcing: bfloat16 [32, 3, 2, 256, 1440], P('ens', None, None, 'lat'), may hold values from -4 to 4
Outputs:
- forecast: float32 [32, 3, 2, 256, 1440], P('ens', None, None, 'lat')
The draws below stay inside these ranges and needn't reach their ends.
Inputs may be any that keep to these rules, and one draw needn't show every extreme that they name: The ancestors of particles g * 4 to (g + 1) * 4 - 1 lie among the last half of 4 particles of group g - 1, the 4 particles of group g and the first half of 4 particles of group g + 1, groups counted cyclically; every group takes at least one ancestor from each of its two neighbouring groups, and in every draw one group takes all its ancestors from its two neighbouring groups.
All inputs are finite; a program needn't handle non-finite values.
Results may differ from the reference program's by a relative error of at most 0.0003.
Values sent between devices are 32-bit elements; how exact they have to be, the bound alone decides.
A program may use at most 128 MiB of HBM per device.

```python
import math
import jax
import jax.numpy as jnp
from jax import lax

PART_DEV = 4
LON = 1440
LAYERS = 2
SUBSTEPS = 3
PARTICLES = 32
NLAT = 256


def draw_ancestors(key, part):
    groups = PARTICLES // PART_DEV
    half_group = PART_DEV // 2
    window_span = 2 * PART_DEV
    key_slots, key_favour, key_picks, key_forced, key_low, key_high, key_order = jax.random.split(key, 7)
    slots = jax.random.randint(key_slots, (groups, PART_DEV), 0, window_span)
    favour = jax.random.randint(key_favour, (groups, 1), 0, window_span)
    picks = jax.random.randint(key_picks, (groups, PART_DEV), 0, 2)
    slots = jnp.where(picks == 1, favour, slots)
    low_slot = jax.random.randint(key_low, (groups,), 0, half_group)
    high_slot = jax.random.randint(key_high, (groups,), window_span - half_group, window_span)
    slots = slots.at[:, 0].set(low_slot)
    slots = slots.at[:, PART_DEV - 1].set(high_slot)
    edges = jnp.concatenate([jnp.arange(half_group), window_span - half_group + jnp.arange(half_group)]).astype(jnp.int32)
    forced_group = jax.random.randint(key_forced, (), 0, groups)
    group_ids = jnp.arange(groups)[:, None]
    slots = jnp.where(group_ids == forced_group, edges[None, :], slots)
    scores = jax.random.randint(key_order, (groups, PART_DEV), 0, 1000) * PART_DEV + jnp.arange(PART_DEV)[None, :]
    order = jnp.argsort(scores, axis=1, stable=True)
    slots = jnp.take_along_axis(slots, order, axis=1)
    window_start = group_ids * PART_DEV - half_group
    return jnp.mod(window_start + slots, PARTICLES).reshape(-1).astype(jnp.int32)


def steps_of(key, shape, shards, low, top_value):
    factor_of, own = 1.0, jax.random.fold_in(key, 6)
    for dim, shards_of in shards:
        steps = jnp.exp(jax.random.uniform(jax.random.fold_in(own, dim), (shards_of,), jnp.float32, low / len(shards), top_value / len(shards)))
        factor_of = factor_of * jnp.repeat(steps, shape[dim] // shards_of).reshape([-1 if axis == dim else 1 for axis in range(len(shape))])
    return factor_of


def scatter_about(stream_key, shape, deviation, most, pieces=(), held_as=jnp.bfloat16):
    array = deviation * jax.random.normal(stream_key, shape, jnp.float32)
    if pieces:
        array = array * steps_of(stream_key, shape, pieces, -0.22, 0.18)
    return jnp.clip(array, -most, most).astype(held_as)


def setup_inputs(seed: int = 0) -> dict:
    streams_of = jax.random.split(jax.random.key(seed), 5)
    ensemble = scatter_about(streams_of[0], (PARTICLES, 3, LAYERS, NLAT, LON), 1.0, 6.0, ((0, 8), (3, 4)), jnp.float32)
    ancestors = draw_ancestors(jax.random.fold_in(streams_of[4], 71), 0)
    depth = jnp.clip(jnp.exp(math.log(1.0) - 1.2039728 * jax.random.uniform(streams_of[2], (LAYERS, NLAT, LON), jnp.float32) ** steps_of(streams_of[2], (LAYERS, NLAT, LON), ((1, 4),), -0.2, 0.2)), 0.3, 1.0)
    forcing = scatter_about(streams_of[3], (PARTICLES, SUBSTEPS, LAYERS, NLAT, LON), 0.3, 4.0, ((0, 8), (3, 4)))
    return {"ensemble": ensemble, "ancestors": ancestors, "depth": depth, "forcing": forcing}


time_step = 0.6
coriolis_peak = 0.5
reduced_gravity = 0.5


def layer_pressure(height, layer_axis):
    layers_here = height.shape[layer_axis]
    shape_ones = [1] * height.ndim
    shape_ones[layer_axis] = layers_here
    weights = (jnp.arange(layers_here) >= 1).astype(height.dtype).reshape(shape_ones)
    lowered = jnp.cumsum(height * weights, axis=layer_axis)
    return jnp.sum(height, axis=layer_axis, keepdims=True) + reduced_gravity * lowered


def coriolis_rows(first_row, count, total_rows):
    row_values = (first_row + jnp.arange(count)).astype(jnp.float32)
    latitude = jnp.pi * ((row_values + 0.5) / total_rows - 0.5)
    return coriolis_peak * jnp.sin(latitude)


def advance(particle_state, depth):
    height, eastward, northward = particle_state[0], particle_state[1], particle_state[2]
    flux_east = depth * eastward
    flux_north = depth * northward
    padded_north = jnp.pad(flux_north, ((0, 0), (1, 1), (0, 0)))
    divergence = (jnp.roll(flux_east, -1, -1) - jnp.roll(flux_east, 1, -1)) * 0.5 + (padded_north[:, 2:] - padded_north[:, :-2]) * 0.5
    height_det = height - time_step * divergence
    pressure = layer_pressure(height_det, 0)
    padded_pressure = jnp.pad(pressure, ((0, 0), (1, 1), (0, 0)))
    slope_east = (jnp.roll(pressure, -1, -1) - jnp.roll(pressure, 1, -1)) * 0.5
    slope_north = (padded_pressure[:, 2:] - padded_pressure[:, :-2]) * 0.5
    coriolis = coriolis_rows(0, NLAT, NLAT)[:, None]
    east_next = eastward + time_step * (coriolis * northward - slope_east)
    north_next = northward + time_step * (-coriolis * east_next - slope_north)
    return jnp.stack([height_det, east_next, north_next])


def reference(ensemble, ancestors, depth, forcing):
    def advance_one(particle):
        source = ancestors[particle].astype(jnp.int32)
        particle_state = lax.dynamic_index_in_dim(ensemble, source, 0, keepdims=False)
        for substep in range(SUBSTEPS):
            particle_state = advance(particle_state, depth)
            particle_state = particle_state.at[0].add(forcing[particle, substep].astype(jnp.float32))
        return particle_state

    return lax.map(advance_one, jnp.arange(PARTICLES, dtype=jnp.int32))
```

```python
import functools

import jax
import jax.numpy as jnp
from jax import lax
from jax.experimental import pallas as pl
from jax.experimental.pallas import tpu as pltpu
from jax.sharding import PartitionSpec as P

SUBSTEPS = 3
time_step = 0.6
coriolis_peak = 0.5
reduced_gravity = 0.5

EDGE = 8
MESH = pl.DeviceIdType.MESH


def coriolis_rows(first_row, count, total_rows):
    row_values = (first_row + jnp.arange(count)).astype(jnp.float32)
    latitude = jnp.pi * ((row_values + 0.5) / total_rows - 0.5)
    return coriolis_peak * jnp.sin(latitude)


def exchange(
    n_ens, n_lat, own, depth, force_lo, force_hi,
    recv, halo_lo, halo_hi, depth_lo, depth_hi, edge_lo, edge_hi,
    send_sem, recv_sem, lat_send, lat_recv,
):
    ens, lat = lax.axis_index("ens"), lax.axis_index("lat")
    nxt, prv = lax.rem(ens + 1, n_ens), lax.rem(ens + n_ens - 1, n_ens)
    part_dev, rows = own.shape[0], own.shape[3]
    half = part_dev // 2
    has_lo, has_hi = lat > 0, lat < n_lat - 1

    barrier = pltpu.get_barrier_semaphore()
    pl.semaphore_signal(barrier, inc=1, device_id=(nxt, lat), device_id_type=MESH)
    pl.semaphore_signal(barrier, inc=1, device_id=(prv, lat), device_id_type=MESH)

    @pl.when(has_lo)
    def _():
        pl.semaphore_signal(barrier, inc=1, device_id=(ens, lat - 1), device_id_type=MESH)

    @pl.when(has_hi)
    def _():
        pl.semaphore_signal(barrier, inc=1, device_id=(ens, lat + 1), device_id_type=MESH)

    pl.semaphore_wait(barrier, 2 + jnp.where(has_lo, 1, 0) + jnp.where(has_hi, 1, 0))

    pieces = ((0, EDGE), (rows - EDGE, EDGE), (EDGE, rows - 2 * EDGE))

    def ens_copies(i):
        at = pl.ds(*pieces[i])
        up = pltpu.make_async_remote_copy(
            src_ref=own.at[pl.ds(half, half), :, :, at, :],
            dst_ref=recv.at[pl.ds(0, half), :, :, at, :],
            send_sem=send_sem.at[2 * i], recv_sem=recv_sem.at[2 * i],
            device_id=(nxt, lat), device_id_type=MESH,
        )
        down = pltpu.make_async_remote_copy(
            src_ref=own.at[pl.ds(0, half), :, :, at, :],
            dst_ref=recv.at[pl.ds(half, half), :, :, at, :],
            send_sem=send_sem.at[2 * i + 1], recv_sem=recv_sem.at[2 * i + 1],
            device_id=(prv, lat), device_id_type=MESH,
        )
        return up, down

    copies = [ens_copies(i) for i in range(3)]
    for pair in copies:
        for c in pair:
            c.start()

    def lat_copies(side):
        at = pl.ds(rows - EDGE, EDGE) if side == 0 else pl.ds(0, EDGE)
        halo, dep, edge = ((halo_lo, depth_lo, edge_lo), (halo_hi, depth_hi, edge_hi))[side]
        force = (force_hi, force_lo)[side]
        pairs = (
            (own.at[:, :, :, at, :], halo.at[pl.ds(half, part_dev)]),
            (depth.at[:, at, :], dep),
            (force, edge),
            (recv.at[pl.ds(0, half), :, :, at, :], halo.at[pl.ds(0, half)]),
            (recv.at[pl.ds(half, half), :, :, at, :], halo.at[pl.ds(half + part_dev, half)]),
        )
        to = (ens, lat + 1) if side == 0 else (ens, lat - 1)
        return [
            pltpu.make_async_remote_copy(
                src_ref=s, dst_ref=d, send_sem=lat_send.at[5 * side + j], recv_sem=lat_recv.at[5 * side + j],
                device_id=to, device_id_type=MESH,
            )
            for j, (s, d) in enumerate(pairs)
        ]

    to_hi, to_lo = lat_copies(0), lat_copies(1)

    @pl.when(has_hi)
    def _():
        for c in to_hi[:3]:
            c.start()

    @pl.when(has_lo)
    def _():
        for c in to_lo[:3]:
            c.start()

    for c in (*copies[0], *copies[1]):
        c.wait_recv()

    @pl.when(has_hi)
    def _():
        for c in to_hi[3:]:
            c.start()

    @pl.when(has_lo)
    def _():
        for c in to_lo[3:]:
            c.start()

    for c in copies[2]:
        c.wait_recv()

    @pl.when(has_hi)
    def _():
        for c in to_hi:
            c.wait_send()
        for c in to_lo:
            c.wait_recv()

    @pl.when(has_lo)
    def _():
        for c in to_lo:
            c.wait_send()
        for c in to_hi:
            c.wait_recv()

    for pair in copies:
        for c in pair:
            c.wait_send()


def substeps(
    n_lat, position, own, recv, halo_lo, halo_hi, depth, depth_lo, depth_hi, forcing, edge_lo, edge_hi, coriolis,
    out, raw, state, press, deep, force, sems,
):
    p = pl.program_id(0)
    parts = pl.num_programs(0)
    lat = lax.axis_index("lat")
    half = recv.shape[0] // 2
    part_dev, rows, lon = own.shape[0], own.shape[3], own.shape[4]
    wide = state.shape[3]
    layers = own.shape[2]
    blocks = (rows + 2 * EDGE) // 8
    total = n_lat * rows

    def fetch(q, slot, act):
        w = position[q]
        body = raw.at[slot, :, :, pl.ds(EDGE, rows), :]

        def go(src, dst, j):
            c = pltpu.make_async_copy(src, dst, sems.at[slot, j])
            (c.start if act else c.wait)()

        if act:
            @pl.when(w < half)
            def _():
                go(recv.at[w], body, 0)

            @pl.when((w >= half) & (w < half + part_dev))
            def _():
                go(own.at[w - half], body, 0)

            @pl.when(w >= half + part_dev)
            def _():
                go(recv.at[w - part_dev], body, 0)
        else:
            go(own.at[0], body, 0)
        go(halo_lo.at[w], raw.at[slot, :, :, pl.ds(0, EDGE), :], 1)
        go(halo_hi.at[w], raw.at[slot, :, :, pl.ds(EDGE + rows, EDGE), :], 2)

    slot = lax.rem(p, 2)

    @pl.when(p == 0)
    def _():
        fetch(0, 0, True)

    @pl.when(p + 1 < parts)
    def _():
        fetch(p + 1, 1 - slot, True)

    lane = lax.broadcasted_iota(jnp.int32, (8, 128), 1)
    row = lax.broadcasted_iota(jnp.int32, (8, wide), 0)
    inside_lo, inside_hi = lat > 0, lat < n_lat - 1
    tail = (lon // 128) * 128
    left = lon - tail

    def put(ref, index, at, value):
        ref[(*index, at, pl.ds(0, lon))] = value
        last = ref[(*index, at, pl.ds(tail, 128))]
        first = ref[(*index, at, pl.ds(0, 128))]
        ref[(*index, at, pl.ds(tail, 128))] = jnp.where(
            lane < left,
            last,
            jnp.where(lane < 128 - left, pltpu.roll(first, left, 1), pltpu.roll(last, 128 - left, 1)),
        )

    def at_block(e):
        return pl.ds(pl.multiple_of(e * 8, 8), 8)

    @pl.when(p == 0)
    def _():
        for k in range(layers):
            put(deep, (k,), pl.ds(0, 8), jnp.where(inside_lo, depth_lo[k], 0.0))
            put(deep, (k,), pl.ds(EDGE + rows, 8), jnp.where(inside_hi, depth_hi[k], 0.0))

            @pl.loop(0, rows // 8)
            def _(e):
                put(deep, (k,), at_block(e + 1), depth[k, at_block(e), :])

    for s in range(SUBSTEPS):
        for k in range(layers):
            if s < SUBSTEPS - 1:
                put(force, (s, k), pl.ds(0, 8), jnp.where(inside_lo, edge_lo[0, s, k], 0.0))
                put(force, (s, k), pl.ds(EDGE + rows, 8), jnp.where(inside_hi, edge_hi[0, s, k], 0.0))
            else:
                force[s, k, pl.ds(0, 8), :] = jnp.zeros((8, wide), jnp.float32)
                force[s, k, pl.ds(EDGE + rows, 8), :] = jnp.zeros((8, wide), jnp.float32)

            @pl.loop(0, rows // 16)
            def _(e):
                both = forcing[0, s, k, pl.ds(pl.multiple_of(e * 16, 16), 16), :].astype(jnp.float32)
                put(force, (s, k), at_block(2 * e + 1), both[:8])
                put(force, (s, k), at_block(2 * e + 2), both[8:])

    fetch(p, slot, False)

    @pl.loop(0, blocks)
    def _(e):
        inside = ((e > 0) | inside_lo) & ((e < blocks - 1) | inside_hi)
        for f in range(3):
            for k in range(layers):
                put(state, (f, k), at_block(e), jnp.where(inside, raw[slot, f, k, at_block(e), :], 0.0))

    def from_below(before, here):
        return pltpu.roll(jnp.where(row == 7, before, here), 1, 0)

    def from_above(after, here):
        return pltpu.roll(jnp.where(row == 0, after, here), 7, 0)

    for s in range(SUBSTEPS):

        @pl.loop(0, blocks)
        def _(e):
            here, before, after = at_block(e), at_block(jnp.maximum(e - 1, 0)), at_block(jnp.minimum(e + 1, blocks - 1))
            inside = ((e > 0) | inside_lo) & ((e < blocks - 1) | inside_hi)
            heights = []
            for k in range(layers):
                east = deep[k, here, :] * state[1, k, here, :]
                north = deep[k, here, :] * state[2, k, here, :]
                below = from_below(deep[k, before, :] * state[2, k, before, :], north)
                above = from_above(deep[k, after, :] * state[2, k, after, :], north)
                divergence = (pltpu.roll(east, wide - 1, 1) - pltpu.roll(east, 1, 1)) * 0.5 + (above - below) * 0.5
                height = state[0, k, here, :] - time_step * divergence
                heights.append(height)
                state[0, k, here, :] = height + force[s, k, here, :]
            base = functools.reduce(jnp.add, heights)
            lowered = jnp.zeros_like(base)
            for k in range(layers):
                if k:
                    lowered = lowered + heights[k]
                press[k, here, :] = jnp.where(inside, base + reduced_gravity * lowered, 0.0)

        final = s == SUBSTEPS - 1

        @pl.loop(1 if final else 0, blocks - 1 if final else blocks)
        def _(e):
            here, before, after = at_block(e), at_block(jnp.maximum(e - 1, 0)), at_block(jnp.minimum(e + 1, blocks - 1))
            inside = ((e > 0) | inside_lo) & ((e < blocks - 1) | inside_hi)
            turn = jnp.concatenate([coriolis[here, :]] * (wide // 128), axis=1)
            for k in range(layers):
                mid = press[k, here, :]
                slope_east = (pltpu.roll(mid, wide - 1, 1) - pltpu.roll(mid, 1, 1)) * 0.5
                slope_north = (from_above(press[k, after, :], mid) - from_below(press[k, before, :], mid)) * 0.5
                north = state[2, k, here, :]
                east_next = state[1, k, here, :] + time_step * (turn * north - slope_east)
                north_next = north + time_step * (-turn * east_next - slope_north)
                if final:
                    to = at_block(e - 1)
                    out[0, 0, k, to, :] = state[0, k, here, :][:, :lon]
                    out[0, 1, k, to, :] = east_next[:, :lon]
                    out[0, 2, k, to, :] = north_next[:, :lon]
                else:
                    state[1, k, here, :] = jnp.where(inside, east_next, 0.0)
                    state[2, k, here, :] = jnp.where(inside, north_next, 0.0)


def on_device(n_ens, n_lat, ensemble, ancestors, depth, forcing):
    part_dev, fields, layers, rows, lon = ensemble.shape
    half = part_dev // 2
    f32 = jnp.float32
    wide = -(-lon // 128) * 128
    any_space = pl.BlockSpec(memory_space=pl.ANY)
    force_lo = forcing[:, : SUBSTEPS - 1, :, :EDGE].astype(f32)
    force_hi = forcing[:, : SUBSTEPS - 1, :, rows - EDGE :].astype(f32)
    halo = jax.ShapeDtypeStruct((2 * part_dev, fields, layers, EDGE, lon), f32)
    depth_edge = jax.ShapeDtypeStruct((layers, EDGE, lon), f32)
    force_edge = jax.ShapeDtypeStruct(force_lo.shape, f32)
    recv, halo_lo, halo_hi, depth_lo, depth_hi, edge_lo, edge_hi = pl.pallas_call(
        functools.partial(exchange, n_ens, n_lat),
        out_shape=(
            jax.ShapeDtypeStruct(ensemble.shape, f32), halo, halo, depth_edge, depth_edge, force_edge, force_edge,
        ),
        in_specs=[any_space] * 4,
        out_specs=(any_space,) * 7,
        scratch_shapes=[
            pltpu.SemaphoreType.DMA((6,)), pltpu.SemaphoreType.DMA((6,)),
            pltpu.SemaphoreType.DMA((10,)), pltpu.SemaphoreType.DMA((10,)),
        ],
        compiler_params=pltpu.CompilerParams(collective_id=0, has_side_effects=True),
        name="exchange",
    )(ensemble, depth, force_lo, force_hi)

    total = part_dev * n_ens
    position = jnp.mod(ancestors - lax.axis_index("ens") * part_dev + half, total)
    turn = coriolis_rows(lax.axis_index("lat") * rows - EDGE, rows + 2 * EDGE, rows * n_lat)
    turn = jnp.broadcast_to(turn[:, None], (rows + 2 * EDGE, 128))
    padded = rows + 2 * EDGE

    def whole(shape):
        return pl.BlockSpec(shape, lambda p, *_: (0,) * len(shape))

    return pl.pallas_call(
        functools.partial(substeps, n_lat),
        out_shape=jax.ShapeDtypeStruct(ensemble.shape, f32),
        grid_spec=pltpu.PrefetchScalarGridSpec(
            num_scalar_prefetch=1,
            grid=(part_dev,),
            in_specs=[
                any_space, any_space, any_space, any_space,
                whole(depth.shape), whole(depth_edge.shape), whole(depth_edge.shape),
                pl.BlockSpec((1, SUBSTEPS, layers, rows, lon), lambda p, *_: (p, 0, 0, 0, 0)),
                pl.BlockSpec((1, *force_edge.shape[1:]), lambda p, *_: (p, 0, 0, 0, 0)),
                pl.BlockSpec((1, *force_edge.shape[1:]), lambda p, *_: (p, 0, 0, 0, 0)),
                whole(turn.shape),
            ],
            out_specs=pl.BlockSpec((1, fields, layers, rows, lon), lambda p, *_: (p, 0, 0, 0, 0)),
            scratch_shapes=[
                pltpu.VMEM((2, fields, layers, padded, lon), f32),
                pltpu.VMEM((fields, layers, padded, wide), f32),
                pltpu.VMEM((layers, padded, wide), f32),
                pltpu.VMEM((layers, padded, wide), f32),
                pltpu.VMEM((SUBSTEPS, layers, padded, wide), f32),
                pltpu.SemaphoreType.DMA((2, 3)),
            ],
        ),
        compiler_params=pltpu.CompilerParams(vmem_limit_bytes=56 * 2**20),
        name="substeps",
    )(
        position, ensemble, recv, halo_lo, halo_hi, depth, depth_lo, depth_hi, forcing, edge_lo, edge_hi, turn
    )


def solution(mesh):
    in_specs = (
        P("ens", None, None, "lat", None),
        P("ens"),
        P(None, "lat", None),
        P("ens", None, None, "lat", None),
    )
    out_specs = P("ens", None, None, "lat", None)
    return jax.shard_map(
        functools.partial(on_device, mesh.shape["ens"], mesh.shape["lat"]),
        mesh=mesh, in_specs=in_specs, out_specs=out_specs, check_vma=False,
    )
```

```python
import functools

import jax
import jax.numpy as jnp
from jax import lax
from jax.experimental import pallas as pl
from jax.experimental.pallas import tpu as pltpu
from jax.sharding import PartitionSpec as P

SUBSTEPS = 3
time_step = 0.6
coriolis_peak = 0.5
reduced_gravity = 0.5

EDGE = 8
MESH = pl.DeviceIdType.MESH


def coriolis_rows(first_row, count, total_rows):
    row_values = (first_row + jnp.arange(count)).astype(jnp.float32)
    latitude = jnp.pi * ((row_values + 0.5) / total_rows - 0.5)
    return coriolis_peak * jnp.sin(latitude)


def forecast_kernel(n_ens, n_lat, *refs):
    own, ancestors, depth, forcing, coriolis, out = refs[:6]
    rows, lon = own.shape[3], own.shape[4]
    chunks = rows // 8
    win = refs[6 : 6 + chunks]
    (
        state, press, deep, force, force_raw, depth_raw, stage_out,
        send_sem, recv_sem, own_sem, raw_sem, lat_send, lat_recv, out_sem,
    ) = refs[6 + chunks :]
    ens, lat = lax.axis_index("ens"), lax.axis_index("lat")
    nxt, prv = lax.rem(ens + 1, n_ens), lax.rem(ens + n_ens - 1, n_ens)
    part_dev, layers = own.shape[0], own.shape[2]
    half = part_dev // 2
    wide = state.shape[4]
    blocks = chunks + 2
    has_lo, has_hi = lat > 0, lat < n_lat - 1

    barrier = pltpu.get_barrier_semaphore()
    pl.semaphore_signal(barrier, inc=1, device_id=(nxt, lat), device_id_type=MESH)
    pl.semaphore_signal(barrier, inc=1, device_id=(prv, lat), device_id_type=MESH)

    @pl.when(has_lo)
    def _():
        pl.semaphore_signal(barrier, inc=1, device_id=(ens, lat - 1), device_id_type=MESH)

    @pl.when(has_hi)
    def _():
        pl.semaphore_signal(barrier, inc=1, device_id=(ens, lat + 1), device_id_type=MESH)

    pl.semaphore_wait(barrier, 2 + jnp.where(has_lo, 1, 0) + jnp.where(has_hi, 1, 0))

    def ens_copies(c):
        at = pl.ds(8 * c, 8)
        up = pltpu.make_async_remote_copy(
            src_ref=own.at[pl.ds(half, half), :, :, at, :], dst_ref=win[c].at[pl.ds(0, half)],
            send_sem=send_sem.at[2 * c], recv_sem=recv_sem.at[2 * c],
            device_id=(nxt, lat), device_id_type=MESH,
        )
        down = pltpu.make_async_remote_copy(
            src_ref=own.at[pl.ds(0, half), :, :, at, :], dst_ref=win[c].at[pl.ds(half + part_dev, half)],
            send_sem=send_sem.at[2 * c + 1], recv_sem=recv_sem.at[2 * c + 1],
            device_id=(prv, lat), device_id_type=MESH,
        )
        return up, down

    def own_copy(c):
        return pltpu.make_async_copy(
            own.at[:, :, :, pl.ds(8 * c, 8), :], win[c].at[pl.ds(half, part_dev)], own_sem.at[c]
        )

    order = (0, chunks - 1, *range(1, chunks - 1))
    for c in order:
        for copy in ens_copies(c):
            copy.start()
    depth_copy = pltpu.make_async_copy(depth, depth_raw, raw_sem.at[0])
    force_copy = pltpu.make_async_copy(forcing, force_raw, raw_sem.at[1])
    depth_copy.start()
    force_copy.start()
    for c in order:
        own_copy(c).start()

    lane = lax.broadcasted_iota(jnp.int32, (8, 128), 1)
    row = lax.broadcasted_iota(jnp.int32, (8, wide), 0)
    tail = (lon // 128) * 128
    left = lon - tail

    def put(ref, index, at, value):
        ref[(*index, at, pl.ds(0, lon))] = value
        last = ref[(*index, at, pl.ds(tail, 128))]
        first = ref[(*index, at, pl.ds(0, 128))]
        ref[(*index, at, pl.ds(tail, 128))] = jnp.where(
            lane < left,
            last,
            jnp.where(lane < 128 - left, pltpu.roll(first, left, 1), pltpu.roll(last, 128 - left, 1)),
        )

    def at_block(e):
        return pl.ds(pl.multiple_of(e * 8, 8), 8)

    top, bottom = pl.ds(0, 8), pl.ds(EDGE + rows, 8)
    first, last = pl.ds(8, 8), pl.ds(rows, 8)
    zero = jnp.zeros((8, wide), jnp.float32)

    def clear(at):
        for k in range(layers):
            deep[k, at, :] = zero

            @pl.loop(0, part_dev)
            def _(p):
                for s in range(SUBSTEPS - 1):
                    force[p, s, k, at, :] = zero
                for f in range(3):
                    state[p, f, k, at, :] = zero

    @pl.when(jnp.logical_not(has_lo))
    def _():
        clear(top)

    @pl.when(jnp.logical_not(has_hi))
    def _():
        clear(bottom)

    def lat_copies(side):
        src, dst = ((last, top), (first, bottom))[side]
        to = (ens, lat + 1) if side == 0 else (ens, lat - 1)
        pairs = (
            (deep.at[:, src, :], deep.at[:, dst, :]),
            (force.at[:, pl.ds(0, SUBSTEPS - 1), :, src, :], force.at[:, pl.ds(0, SUBSTEPS - 1), :, dst, :]),
            (state.at[:, :, :, src, :], state.at[:, :, :, dst, :]),
        )
        return [
            pltpu.make_async_remote_copy(
                src_ref=s, dst_ref=d, send_sem=lat_send.at[3 * side + j], recv_sem=lat_recv.at[3 * side + j],
                device_id=to, device_id_type=MESH,
            )
            for j, (s, d) in enumerate(pairs)
        ]

    to_hi, to_lo = lat_copies(0), lat_copies(1)

    def lat_start(lo, hi):
        @pl.when(has_hi)
        def _():
            for c in to_hi[lo:hi]:
                c.start()

        @pl.when(has_lo)
        def _():
            for c in to_lo[lo:hi]:
                c.start()

    depth_copy.wait()

    @pl.loop(0, chunks)
    def _(c):
        for k in range(layers):
            put(deep, (k,), at_block(c + 1), depth_raw[k, at_block(c), :])

    force_copy.wait()

    @pl.loop(0, part_dev)
    def _(p):
        for s in range(SUBSTEPS):
            for k in range(layers):
                if s == SUBSTEPS - 1:
                    force[p, s, k, top, :] = zero
                    force[p, s, k, bottom, :] = zero

                @pl.loop(0, rows // 16)
                def _(e):
                    both = force_raw[p, s, k, pl.ds(pl.multiple_of(e * 16, 16), 16), :].astype(jnp.float32)
                    put(force, (p, s, k), at_block(2 * e + 1), both[:8])
                    put(force, (p, s, k), at_block(2 * e + 2), both[8:])

    lat_start(0, 2)

    def take(c):
        for copy in ens_copies(c):
            copy.wait_recv()
        own_copy(c).wait()

        @pl.loop(0, part_dev)
        def _(p):
            w = lax.rem(ancestors[p] - ens * part_dev + half + n_ens * part_dev, n_ens * part_dev)
            w = jnp.minimum(w, 2 * part_dev - 1)
            for f in range(3):
                for k in range(layers):
                    put(state, (p, f, k), pl.ds(8 * c + 8, 8), win[c][w, f, k, :, :])

    take(0)
    take(chunks - 1)
    lat_start(2, 3)

    @pl.when(has_hi)
    def _():
        for c in to_hi:
            c.wait_send()
        for c in to_lo:
            c.wait_recv()

    @pl.when(has_lo)
    def _():
        for c in to_lo:
            c.wait_send()
        for c in to_hi:
            c.wait_recv()

    def from_below(before, here):
        return pltpu.roll(jnp.where(row == 7, before, here), 1, 0)

    def from_above(after, here):
        return pltpu.roll(jnp.where(row == 0, after, here), 7, 0)

    def around(e):
        inside = ((e > 0) | has_lo) & ((e < blocks - 1) | has_hi)
        return at_block(e), at_block(jnp.maximum(e - 1, 0)), at_block(jnp.minimum(e + 1, blocks - 1)), inside

    def heights_of(p, s, e):
        here, before, after, inside = around(e)
        heights = []
        for k in range(layers):
            east = deep[k, here, :] * state[p, 1, k, here, :]
            north = deep[k, here, :] * state[p, 2, k, here, :]
            below = from_below(deep[k, before, :] * state[p, 2, k, before, :], north)
            above = from_above(deep[k, after, :] * state[p, 2, k, after, :], north)
            divergence = (pltpu.roll(east, wide - 1, 1) - pltpu.roll(east, 1, 1)) * 0.5 + (above - below) * 0.5
            height = state[p, 0, k, here, :] - time_step * divergence
            heights.append(height)
            state[p, 0, k, here, :] = height + force[p, s, k, here, :]
        base = functools.reduce(jnp.add, heights)
        lowered = jnp.zeros_like(base)
        for k in range(layers):
            if k:
                lowered = lowered + heights[k]
            press[p, k, here, :] = jnp.where(inside, base + reduced_gravity * lowered, 0.0)

    def velocities(p, e, final):
        here, before, after, inside = around(e)
        turn = jnp.concatenate([coriolis[here, :]] * (wide // 128), axis=1)
        slot = lax.rem(e, 2)
        for k in range(layers):
            mid = press[p, k, here, :]
            slope_east = (pltpu.roll(mid, wide - 1, 1) - pltpu.roll(mid, 1, 1)) * 0.5
            slope_north = (from_above(press[p, k, after, :], mid) - from_below(press[p, k, before, :], mid)) * 0.5
            north = state[p, 2, k, here, :]
            east_next = state[p, 1, k, here, :] + time_step * (turn * north - slope_east)
            north_next = north + time_step * (-turn * east_next - slope_north)
            if final:
                stage_out[slot, p, 0, k, :, :] = state[p, 0, k, here, :][:, :lon]
                stage_out[slot, p, 1, k, :, :] = east_next[:, :lon]
                stage_out[slot, p, 2, k, :, :] = north_next[:, :lon]
            else:
                state[p, 1, k, here, :] = jnp.where(inside, east_next, 0.0)
                state[p, 2, k, here, :] = jnp.where(inside, north_next, 0.0)

    def out_copy(e):
        slot = lax.rem(e, 2)
        return pltpu.make_async_copy(stage_out.at[slot], out.at[:, :, :, at_block(e - 1), :], out_sem.at[slot])

    @pl.loop(0, blocks + 2 * SUBSTEPS - 2)
    def _(step):
        for c in range(1, chunks - 1):

            @pl.when(step == c)
            def _():
                take(c)

        @pl.loop(0, SUBSTEPS)
        def _(s):
            e = step - 2 * s

            @pl.when((e >= 0) & (e < blocks))
            def _():
                @pl.loop(0, part_dev)
                def _(p):
                    heights_of(p, s, e)

            j = e - 1

            @pl.when((j >= 0) & (j < blocks) & (s < SUBSTEPS - 1))
            def _():
                @pl.loop(0, part_dev)
                def _(p):
                    velocities(p, j, False)

        j = step - 2 * SUBSTEPS + 1

        @pl.when((j >= 1) & (j < blocks - 1))
        def _():
            @pl.when(j >= 3)
            def _():
                out_copy(j - 2).wait()

            @pl.loop(0, part_dev)
            def _(p):
                velocities(p, j, True)

            out_copy(j).start()

    out_copy(blocks - 3).wait()
    out_copy(blocks - 2).wait()
    for c in order:
        for copy in ens_copies(c):
            copy.wait_send()


def on_device(n_ens, n_lat, ensemble, ancestors, depth, forcing):
    part_dev, fields, layers, rows, lon = ensemble.shape
    f32 = jnp.float32
    wide = -(-lon // 128) * 128
    padded = rows + 2 * EDGE
    chunks = rows // 8
    any_space = pl.BlockSpec(memory_space=pl.ANY)
    turn = coriolis_rows(lax.axis_index("lat") * rows - EDGE, padded, rows * n_lat)
    turn = jnp.broadcast_to(turn[:, None], (padded, 128))
    dma = pltpu.SemaphoreType.DMA
    return pl.pallas_call(
        functools.partial(forecast_kernel, n_ens, n_lat),
        out_shape=jax.ShapeDtypeStruct(ensemble.shape, f32),
        in_specs=[
            any_space, pl.BlockSpec(memory_space=pltpu.SMEM), any_space, any_space,
            pl.BlockSpec(memory_space=pltpu.VMEM),
        ],
        out_specs=any_space,
        scratch_shapes=[
            *[pltpu.VMEM((2 * part_dev, fields, layers, 8, lon), f32) for _ in range(chunks)],
            pltpu.VMEM((part_dev, fields, layers, padded, wide), f32),
            pltpu.VMEM((part_dev, layers, padded, wide), f32),
            pltpu.VMEM((layers, padded, wide), f32),
            pltpu.VMEM((part_dev, SUBSTEPS, layers, padded, wide), f32),
            pltpu.VMEM(forcing.shape, forcing.dtype),
            pltpu.VMEM(depth.shape, f32),
            pltpu.VMEM((2, part_dev, fields, layers, 8, lon), f32),
            dma((2 * chunks,)), dma((2 * chunks,)), dma((chunks,)), dma((2,)), dma((6,)), dma((6,)), dma((2,)),
        ],
        compiler_params=pltpu.CompilerParams(
            collective_id=0, has_side_effects=True, vmem_limit_bytes=60 * 2**20
        ),
        name="forecast",
    )(ensemble, ancestors, depth, forcing, turn)


def solution(mesh):
    in_specs = (
        P("ens", None, None, "lat", None),
        P("ens"),
        P(None, "lat", None),
        P("ens", None, None, "lat", None),
    )
    out_specs = P("ens", None, None, "lat", None)
    return jax.shard_map(
        functools.partial(on_device, mesh.shape["ens"], mesh.shape["lat"]),
        mesh=mesh, in_specs=in_specs, out_specs=out_specs, check_vma=False,
    )
```

```python
import functools

import jax
import jax.numpy as jnp
from jax import lax
from jax.experimental import pallas as pl
from jax.experimental.pallas import tpu as pltpu
from jax.sharding import PartitionSpec as P

SUBSTEPS = 3
time_step = 0.6
coriolis_peak = 0.5
reduced_gravity = 0.5

EDGE = 8
MESH = pl.DeviceIdType.MESH


def coriolis_rows(first_row, count, total_rows):
    row_values = (first_row + jnp.arange(count)).astype(jnp.float32)
    latitude = jnp.pi * ((row_values + 0.5) / total_rows - 0.5)
    return coriolis_peak * jnp.sin(latitude)


def forecast_kernel(n_ens, n_lat, *refs):
    own, ancestors, depth, forcing, coriolis, out = refs[:6]
    rows, lon = own.shape[3], own.shape[4]
    chunks = rows // 8
    win = refs[6 : 6 + chunks]
    (
        state, press, deep, force, force_raw, depth_raw, stage_out,
        send_sem, recv_sem, own_sem, raw_sem, lat_send, lat_recv, out_sem,
    ) = refs[6 + chunks :]
    ens, lat = lax.axis_index("ens"), lax.axis_index("lat")
    nxt, prv = lax.rem(ens + 1, n_ens), lax.rem(ens + n_ens - 1, n_ens)
    part_dev, layers = own.shape[0], own.shape[2]
    half = part_dev // 2
    wide = state.shape[4]
    blocks = chunks + 2
    has_lo, has_hi = lat > 0, lat < n_lat - 1

    barrier = pltpu.get_barrier_semaphore()
    pl.semaphore_signal(barrier, inc=1, device_id=(nxt, lat), device_id_type=MESH)
    pl.semaphore_signal(barrier, inc=1, device_id=(prv, lat), device_id_type=MESH)

    @pl.when(has_lo)
    def _():
        pl.semaphore_signal(barrier, inc=1, device_id=(ens, lat - 1), device_id_type=MESH)

    @pl.when(has_hi)
    def _():
        pl.semaphore_signal(barrier, inc=1, device_id=(ens, lat + 1), device_id_type=MESH)

    pl.semaphore_wait(barrier, 2 + jnp.where(has_lo, 1, 0) + jnp.where(has_hi, 1, 0))

    def ens_copies(c):
        at = pl.ds(8 * c, 8)
        up = pltpu.make_async_remote_copy(
            src_ref=own.at[pl.ds(half, half), :, :, at, :], dst_ref=win[c].at[pl.ds(0, half)],
            send_sem=send_sem.at[2 * c], recv_sem=recv_sem.at[2 * c],
            device_id=(nxt, lat), device_id_type=MESH,
        )
        down = pltpu.make_async_remote_copy(
            src_ref=own.at[pl.ds(0, half), :, :, at, :], dst_ref=win[c].at[pl.ds(half + part_dev, half)],
            send_sem=send_sem.at[2 * c + 1], recv_sem=recv_sem.at[2 * c + 1],
            device_id=(prv, lat), device_id_type=MESH,
        )
        return up, down

    def own_copy(c):
        return pltpu.make_async_copy(
            own.at[:, :, :, pl.ds(8 * c, 8), :], win[c].at[pl.ds(half, part_dev)], own_sem.at[c]
        )

    order = (0, chunks - 1, *range(1, chunks - 1))
    for c in order:
        for copy in ens_copies(c):
            copy.start()
    depth_copy = pltpu.make_async_copy(depth, depth_raw, raw_sem.at[0])
    force_copy = pltpu.make_async_copy(forcing, force_raw, raw_sem.at[1])
    depth_copy.start()
    force_copy.start()
    for c in order:
        own_copy(c).start()

    lane = lax.broadcasted_iota(jnp.int32, (8, 128), 1)
    row = lax.broadcasted_iota(jnp.int32, (8, wide), 0)
    tail = (lon // 128) * 128
    left = lon - tail

    def put(ref, index, at, value):
        ref[(*index, at, pl.ds(0, lon))] = value
        last = ref[(*index, at, pl.ds(tail, 128))]
        first = ref[(*index, at, pl.ds(0, 128))]
        ref[(*index, at, pl.ds(tail, 128))] = jnp.where(
            lane < left,
            last,
            jnp.where(lane < 128 - left, pltpu.roll(first, left, 1), pltpu.roll(last, 128 - left, 1)),
        )

    def at_block(e):
        return pl.ds(pl.multiple_of(e * 8, 8), 8)

    top, bottom = pl.ds(0, 8), pl.ds(EDGE + rows, 8)
    first, last = pl.ds(8, 8), pl.ds(rows, 8)
    zero = jnp.zeros((8, wide), jnp.float32)

    def clear(at):
        for k in range(layers):
            deep[k, at, :] = zero

            @pl.loop(0, part_dev)
            def _(p):
                for s in range(SUBSTEPS - 1):
                    force[p, s, k, at, :] = zero
                for f in range(3):
                    state[p, f, k, at, :] = zero

    @pl.when(jnp.logical_not(has_lo))
    def _():
        clear(top)

    @pl.when(jnp.logical_not(has_hi))
    def _():
        clear(bottom)

    def lat_copies(side):
        src, dst = ((last, top), (first, bottom))[side]
        to = (ens, lat + 1) if side == 0 else (ens, lat - 1)
        pairs = (
            (deep.at[:, src, :], deep.at[:, dst, :]),
            (force.at[:, pl.ds(0, SUBSTEPS - 1), :, src, :], force.at[:, pl.ds(0, SUBSTEPS - 1), :, dst, :]),
            (state.at[:, :, :, src, :], state.at[:, :, :, dst, :]),
        )
        return [
            pltpu.make_async_remote_copy(
                src_ref=s, dst_ref=d, send_sem=lat_send.at[3 * side + j], recv_sem=lat_recv.at[3 * side + j],
                device_id=to, device_id_type=MESH,
            )
            for j, (s, d) in enumerate(pairs)
        ]

    to_hi, to_lo = lat_copies(0), lat_copies(1)

    def lat_start(lo, hi):
        @pl.when(has_hi)
        def _():
            for c in to_hi[lo:hi]:
                c.start()

        @pl.when(has_lo)
        def _():
            for c in to_lo[lo:hi]:
                c.start()

    depth_copy.wait()

    @pl.loop(0, chunks)
    def _(c):
        for k in range(layers):
            put(deep, (k,), at_block(c + 1), depth_raw[k, at_block(c), :])

    force_copy.wait()

    @pl.loop(0, part_dev)
    def _(p):
        for s in range(SUBSTEPS):
            for k in range(layers):
                if s == SUBSTEPS - 1:
                    force[p, s, k, top, :] = zero
                    force[p, s, k, bottom, :] = zero

                @pl.loop(0, rows // 16)
                def _(e):
                    both = force_raw[p, s, k, pl.ds(pl.multiple_of(e * 16, 16), 16), :].astype(jnp.float32)
                    put(force, (p, s, k), at_block(2 * e + 1), both[:8])
                    put(force, (p, s, k), at_block(2 * e + 2), both[8:])

    lat_start(0, 2)

    def take(c):
        for copy in ens_copies(c):
            copy.wait_recv()
        own_copy(c).wait()

        @pl.loop(0, part_dev)
        def _(p):
            w = lax.rem(ancestors[p] - ens * part_dev + half + n_ens * part_dev, n_ens * part_dev)
            w = jnp.minimum(w, 2 * part_dev - 1)
            for f in range(3):
                for k in range(layers):
                    put(state, (p, f, k), pl.ds(8 * c + 8, 8), win[c][w, f, k, :, :])

    take(0)
    take(chunks - 1)
    lat_start(2, 3)

    @pl.when(has_hi)
    def _():
        for c in to_hi:
            c.wait_send()
        for c in to_lo:
            c.wait_recv()

    @pl.when(has_lo)
    def _():
        for c in to_lo:
            c.wait_send()
        for c in to_hi:
            c.wait_recv()

    def inside_of(e, c):
        at = e * 8 + c + row
        return ((at >= EDGE) | has_lo) & ((at < EDGE + rows) | has_hi)

    def load(ref, index, e, c):
        low = c % 8
        return ref.at[(*index, pl.ds(pl.multiple_of((e + c // 8) * 8, 8), 16 if low else 8))][low : low + 8, :]

    def save(ref, index, e, c, value):
        low = c % 8
        ref.at[(*index, pl.ds(pl.multiple_of((e + c // 8) * 8, 8), 16 if low else 8))][low : low + 8, :] = value

    def heights_of(p, s, e, c):
        heights = []
        for k in range(layers):
            east = load(deep, (k,), e, c) * load(state, (p, 1, k), e, c)
            below = load(deep, (k,), e, c - 1) * load(state, (p, 2, k), e, c - 1)
            above = load(deep, (k,), e, c + 1) * load(state, (p, 2, k), e, c + 1)
            divergence = (pltpu.roll(east, wide - 1, 1) - pltpu.roll(east, 1, 1)) * 0.5 + (above - below) * 0.5
            height = load(state, (p, 0, k), e, c) - time_step * divergence
            heights.append(height)
            save(state, (p, 0, k), e, c, height + load(force, (p, s, k), e, c))
        base = functools.reduce(jnp.add, heights)
        lowered = jnp.zeros_like(base)
        inside = inside_of(e, c)
        for k in range(layers):
            if k:
                lowered = lowered + heights[k]
            save(press, (p, k), e, c + 8, jnp.where(inside, base + reduced_gravity * lowered, 0.0))

    def velocities(p, e, c):
        inside = inside_of(e, c)
        turn = jnp.concatenate([load(coriolis, (), e, c)] * (wide // 128), axis=1)
        for k in range(layers):
            mid = load(press, (p, k), e, c + 8)
            slope_east = (pltpu.roll(mid, wide - 1, 1) - pltpu.roll(mid, 1, 1)) * 0.5
            slope_north = (load(press, (p, k), e, c + 9) - load(press, (p, k), e, c + 7)) * 0.5
            north = load(state, (p, 2, k), e, c)
            east_next = load(state, (p, 1, k), e, c) + time_step * (turn * north - slope_east)
            north_next = north + time_step * (-turn * east_next - slope_north)
            save(state, (p, 1, k), e, c, jnp.where(inside, east_next, 0.0))
            save(state, (p, 2, k), e, c, jnp.where(inside, north_next, 0.0))

    def out_copy(e):
        slot = lax.rem(e, 2)
        return pltpu.make_async_copy(stage_out.at[slot], out.at[:, :, :, at_block(e - 1), :], out_sem.at[slot])

    @pl.loop(0, blocks)
    def _(e):
        for c in range(1, chunks - 1):

            @pl.when(e == c)
            def _():
                take(c)

        for s in range(SUBSTEPS):

            def substep():
                @pl.loop(0, part_dev)
                def _(p):
                    heights_of(p, s, e, 3 - 2 * s)

                @pl.loop(0, part_dev)
                def _(p):
                    velocities(p, e, 2 - 2 * s)

            if s < 2:
                substep()
            else:
                pl.when(e >= 1)(substep)

        j = e - 1

        @pl.when(j >= 1)
        def _():
            @pl.when(j >= 3)
            def _():
                out_copy(j - 2).wait()

            @pl.loop(0, part_dev)
            def _(p):
                for f in range(3):
                    for k in range(layers):
                        stage_out[lax.rem(j, 2), p, f, k, :, :] = state[p, f, k, at_block(j), pl.ds(0, lon)]

            out_copy(j).start()

    out_copy(blocks - 3).wait()
    out_copy(blocks - 2).wait()
    for c in order:
        for copy in ens_copies(c):
            copy.wait_send()


def on_device(n_ens, n_lat, ensemble, ancestors, depth, forcing):
    part_dev, fields, layers, rows, lon = ensemble.shape
    f32 = jnp.float32
    wide = -(-lon // 128) * 128
    padded = rows + 3 * EDGE
    chunks = rows // 8
    any_space = pl.BlockSpec(memory_space=pl.ANY)
    turn = coriolis_rows(lax.axis_index("lat") * rows - EDGE, padded, rows * n_lat)
    turn = jnp.broadcast_to(turn[:, None], (padded, 128))
    dma = pltpu.SemaphoreType.DMA
    return pl.pallas_call(
        functools.partial(forecast_kernel, n_ens, n_lat),
        out_shape=jax.ShapeDtypeStruct(ensemble.shape, f32),
        in_specs=[
            any_space, pl.BlockSpec(memory_space=pltpu.SMEM), any_space, any_space,
            pl.BlockSpec(memory_space=pltpu.VMEM),
        ],
        out_specs=any_space,
        scratch_shapes=[
            *[pltpu.VMEM((2 * part_dev, fields, layers, 8, lon), f32) for _ in range(chunks)],
            pltpu.VMEM((part_dev, fields, layers, padded, wide), f32),
            pltpu.VMEM((part_dev, layers, padded + 8, wide), f32),
            pltpu.VMEM((layers, padded, wide), f32),
            pltpu.VMEM((part_dev, SUBSTEPS, layers, padded, wide), f32),
            pltpu.VMEM(forcing.shape, forcing.dtype),
            pltpu.VMEM(depth.shape, f32),
            pltpu.VMEM((2, part_dev, fields, layers, 8, lon), f32),
            dma((2 * chunks,)), dma((2 * chunks,)), dma((chunks,)), dma((2,)), dma((6,)), dma((6,)), dma((2,)),
        ],
        compiler_params=pltpu.CompilerParams(
            collective_id=0, has_side_effects=True, vmem_limit_bytes=60 * 2**20
        ),
        name="forecast",
    )(ensemble, ancestors, depth, forcing, turn)


def solution(mesh):
    in_specs = (
        P("ens", None, None, "lat", None),
        P("ens"),
        P(None, "lat", None),
        P("ens", None, None, "lat", None),
    )
    out_specs = P("ens", None, None, "lat", None)
    return jax.shard_map(
        functools.partial(on_device, mesh.shape["ens"], mesh.shape["lat"]),
        mesh=mesh, in_specs=in_specs, out_specs=out_specs, check_vma=False,
    )
```

```python
import functools

import jax
import jax.numpy as jnp
from jax import lax
from jax.experimental import pallas as pl
from jax.experimental.pallas import tpu as pltpu
from jax.sharding import PartitionSpec as P

SUBSTEPS = 3
time_step = 0.6
coriolis_peak = 0.5
reduced_gravity = 0.5

EDGE = 8
MESH = pl.DeviceIdType.MESH


def coriolis_rows(first_row, count, total_rows):
    row_values = (first_row + jnp.arange(count)).astype(jnp.float32)
    latitude = jnp.pi * ((row_values + 0.5) / total_rows - 0.5)
    return coriolis_peak * jnp.sin(latitude)


def forecast_kernel(n_ens, n_lat, *refs):
    own, ancestors, depth, forcing, coriolis, out = refs[:6]
    rows, lon = own.shape[3], own.shape[4]
    chunks = rows // 8
    win = refs[6 : 6 + chunks]
    (
        state, press, deep, force, force_raw, depth_raw, stage_out,
        send_sem, recv_sem, own_sem, raw_sem, lat_send, lat_recv, out_sem,
    ) = refs[6 + chunks :]
    ens, lat = lax.axis_index("ens"), lax.axis_index("lat")
    nxt, prv = lax.rem(ens + 1, n_ens), lax.rem(ens + n_ens - 1, n_ens)
    part_dev, layers = own.shape[0], own.shape[2]
    half = part_dev // 2
    wide = state.shape[4]
    blocks = chunks + 2
    has_lo, has_hi = lat > 0, lat < n_lat - 1

    barrier = pltpu.get_barrier_semaphore()
    pl.semaphore_signal(barrier, inc=1, device_id=(nxt, lat), device_id_type=MESH)
    pl.semaphore_signal(barrier, inc=1, device_id=(prv, lat), device_id_type=MESH)

    @pl.when(has_lo)
    def _():
        pl.semaphore_signal(barrier, inc=1, device_id=(ens, lat - 1), device_id_type=MESH)

    @pl.when(has_hi)
    def _():
        pl.semaphore_signal(barrier, inc=1, device_id=(ens, lat + 1), device_id_type=MESH)

    pl.semaphore_wait(barrier, 2 + jnp.where(has_lo, 1, 0) + jnp.where(has_hi, 1, 0))

    def ens_copies(c):
        at = pl.ds(8 * c, 8)
        up = pltpu.make_async_remote_copy(
            src_ref=own.at[pl.ds(half, half), :, :, at, :], dst_ref=win[c].at[pl.ds(0, half)],
            send_sem=send_sem.at[2 * c], recv_sem=recv_sem.at[2 * c],
            device_id=(nxt, lat), device_id_type=MESH,
        )
        down = pltpu.make_async_remote_copy(
            src_ref=own.at[pl.ds(0, half), :, :, at, :], dst_ref=win[c].at[pl.ds(half + part_dev, half)],
            send_sem=send_sem.at[2 * c + 1], recv_sem=recv_sem.at[2 * c + 1],
            device_id=(prv, lat), device_id_type=MESH,
        )
        return up, down

    def own_copy(c):
        return pltpu.make_async_copy(
            own.at[:, :, :, pl.ds(8 * c, 8), :], win[c].at[pl.ds(half, part_dev)], own_sem.at[c]
        )

    order = (0, chunks - 1, *range(1, chunks - 1))
    for c in order:
        for copy in ens_copies(c):
            copy.start()
    depth_copy = pltpu.make_async_copy(depth, depth_raw, raw_sem.at[0])
    force_copy = pltpu.make_async_copy(forcing, force_raw, raw_sem.at[1])
    depth_copy.start()
    force_copy.start()
    for c in order:
        own_copy(c).start()

    lane = lax.broadcasted_iota(jnp.int32, (8, 128), 1)
    row = lax.broadcasted_iota(jnp.int32, (8, wide), 0)
    tail = (lon // 128) * 128
    left = lon - tail

    def put(ref, index, at, value):
        ref[(*index, at, pl.ds(0, lon))] = value
        last = ref[(*index, at, pl.ds(tail, 128))]
        first = ref[(*index, at, pl.ds(0, 128))]
        ref[(*index, at, pl.ds(tail, 128))] = jnp.where(
            lane < left,
            last,
            jnp.where(lane < 128 - left, pltpu.roll(first, left, 1), pltpu.roll(last, 128 - left, 1)),
        )

    def at_block(e):
        return pl.ds(pl.multiple_of(e * 8, 8), 8)

    top, bottom = pl.ds(0, 8), pl.ds(EDGE + rows, 8)
    first, last = pl.ds(8, 8), pl.ds(rows, 8)
    zero = jnp.zeros((8, wide), jnp.float32)

    def clear(at):
        for k in range(layers):
            deep[k, at, :] = zero

            @pl.loop(0, part_dev)
            def _(p):
                for s in range(SUBSTEPS - 1):
                    force[p, s, k, at, :] = zero
                for f in range(3):
                    state[p, f, k, at, :] = zero

    @pl.when(jnp.logical_not(has_lo))
    def _():
        clear(top)

    @pl.when(jnp.logical_not(has_hi))
    def _():
        clear(bottom)

    def lat_copies(side):
        src, dst = ((last, top), (first, bottom))[side]
        to = (ens, lat + 1) if side == 0 else (ens, lat - 1)
        pairs = (
            (deep.at[:, src, :], deep.at[:, dst, :]),
            (force.at[:, pl.ds(0, SUBSTEPS - 1), :, src, :], force.at[:, pl.ds(0, SUBSTEPS - 1), :, dst, :]),
            (state.at[:, :, :, src, :], state.at[:, :, :, dst, :]),
        )
        return [
            pltpu.make_async_remote_copy(
                src_ref=s, dst_ref=d, send_sem=lat_send.at[3 * side + j], recv_sem=lat_recv.at[3 * side + j],
                device_id=to, device_id_type=MESH,
            )
            for j, (s, d) in enumerate(pairs)
        ]

    to_hi, to_lo = lat_copies(0), lat_copies(1)

    def lat_start(lo, hi):
        @pl.when(has_hi)
        def _():
            for c in to_hi[lo:hi]:
                c.start()

        @pl.when(has_lo)
        def _():
            for c in to_lo[lo:hi]:
                c.start()

    depth_copy.wait()

    @pl.loop(0, chunks)
    def _(c):
        for k in range(layers):
            put(deep, (k,), at_block(c + 1), depth_raw[k, at_block(c), :])

    force_copy.wait()

    @pl.loop(0, part_dev)
    def _(p):
        for s in range(SUBSTEPS):
            for k in range(layers):
                if s == SUBSTEPS - 1:
                    force[p, s, k, top, :] = zero
                    force[p, s, k, bottom, :] = zero

                @pl.loop(0, rows // 16)
                def _(e):
                    both = force_raw[p, s, k, pl.ds(pl.multiple_of(e * 16, 16), 16), :].astype(jnp.float32)
                    put(force, (p, s, k), at_block(2 * e + 1), both[:8])
                    put(force, (p, s, k), at_block(2 * e + 2), both[8:])

    lat_start(0, 2)

    def take(c):
        for copy in ens_copies(c):
            copy.wait_recv()
        own_copy(c).wait()

        @pl.loop(0, part_dev)
        def _(p):
            w = lax.rem(ancestors[p] - ens * part_dev + half + n_ens * part_dev, n_ens * part_dev)
            w = jnp.minimum(w, 2 * part_dev - 1)
            for f in range(3):
                for k in range(layers):
                    put(state, (p, f, k), pl.ds(8 * c + 8, 8), win[c][w, f, k, :, :])

    take(0)
    take(chunks - 1)
    lat_start(2, 3)

    @pl.when(has_hi)
    def _():
        for c in to_hi:
            c.wait_send()
        for c in to_lo:
            c.wait_recv()

    @pl.when(has_lo)
    def _():
        for c in to_lo:
            c.wait_send()
        for c in to_hi:
            c.wait_recv()

    def inside_of(e, c):
        at = e * 8 + c + row
        return ((at >= EDGE) | has_lo) & ((at < EDGE + rows) | has_hi)

    def load(ref, index, e, c):
        low = c % 8
        return ref.at[(*index, pl.ds(pl.multiple_of((e + c // 8) * 8, 8), 16 if low else 8))][low : low + 8, :]

    def save(ref, index, e, c, value):
        low = c % 8
        ref.at[(*index, pl.ds(pl.multiple_of((e + c // 8) * 8, 8), 16 if low else 8))][low : low + 8, :] = value

    def heights_of(p, s, e, c):
        heights = []
        for k in range(layers):
            east = load(deep, (k,), e, c) * load(state, (p, 1, k), e, c)
            below = load(deep, (k,), e, c - 1) * load(state, (p, 2, k), e, c - 1)
            above = load(deep, (k,), e, c + 1) * load(state, (p, 2, k), e, c + 1)
            divergence = (pltpu.roll(east, wide - 1, 1) - pltpu.roll(east, 1, 1)) * 0.5 + (above - below) * 0.5
            height = load(state, (p, 0, k), e, c) - time_step * divergence
            heights.append(height)
            save(state, (p, 0, k), e, c, height + load(force, (p, s, k), e, c))
        base = functools.reduce(jnp.add, heights)
        lowered = jnp.zeros_like(base)
        inside = inside_of(e, c)
        for k in range(layers):
            if k:
                lowered = lowered + heights[k]
            save(press, (p, k), e, c + 8, jnp.where(inside, base + reduced_gravity * lowered, 0.0))

    def velocities(p, e, c):
        inside = inside_of(e, c)
        turn = jnp.concatenate([load(coriolis, (), e, c)] * (wide // 128), axis=1)
        for k in range(layers):
            mid = load(press, (p, k), e, c + 8)
            slope_east = (pltpu.roll(mid, wide - 1, 1) - pltpu.roll(mid, 1, 1)) * 0.5
            slope_north = (load(press, (p, k), e, c + 9) - load(press, (p, k), e, c + 7)) * 0.5
            north = load(state, (p, 2, k), e, c)
            east_next = load(state, (p, 1, k), e, c) + time_step * (turn * north - slope_east)
            north_next = north + time_step * (-turn * east_next - slope_north)
            save(state, (p, 1, k), e, c, jnp.where(inside, east_next, 0.0))
            save(state, (p, 2, k), e, c, jnp.where(inside, north_next, 0.0))

    def out_copy(e):
        slot = lax.rem(e, 2)
        return pltpu.make_async_copy(stage_out.at[slot], out.at[:, :, :, at_block(e - 1), :], out_sem.at[slot])

    @pl.loop(0, blocks)
    def _(e):
        for c in range(1, chunks - 1):

            @pl.when(e == c)
            def _():
                take(c)

        for s in range(SUBSTEPS):

            def substep():
                @pl.loop(0, part_dev)
                def _(p):
                    heights_of(p, s, e, 3 - 2 * s)

                @pl.loop(0, part_dev)
                def _(p):
                    velocities(p, e, 2 - 2 * s)

            if s < 2:
                substep()
            else:
                pl.when(e >= 1)(substep)

        j = e - 1

        @pl.when(j >= 1)
        def _():
            @pl.when(j >= 3)
            def _():
                out_copy(j - 2).wait()

            @pl.loop(0, part_dev)
            def _(p):
                for f in range(3):
                    for k in range(layers):
                        stage_out[lax.rem(j, 2), p, f, k, :, :] = state[p, f, k, at_block(j), pl.ds(0, lon)]

            out_copy(j).start()

    out_copy(blocks - 3).wait()
    out_copy(blocks - 2).wait()
    for c in order:
        for copy in ens_copies(c):
            copy.wait_send()


def hand_over(source, target):
    target[...] = source[...]


def on_device(n_ens, n_lat, ensemble, ancestors, depth, forcing):
    part_dev, fields, layers, rows, lon = ensemble.shape
    f32 = jnp.float32
    wide = -(-lon // 128) * 128
    padded = rows + 3 * EDGE
    chunks = rows // 8
    any_space = pl.BlockSpec(memory_space=pl.ANY)
    turn = coriolis_rows(lax.axis_index("lat") * rows - EDGE, padded, rows * n_lat)
    turn = jnp.broadcast_to(turn[:, None], (padded, 128))
    dma = pltpu.SemaphoreType.DMA
    result = pl.pallas_call(
        functools.partial(forecast_kernel, n_ens, n_lat),
        out_shape=jax.ShapeDtypeStruct(ensemble.shape, f32),
        in_specs=[
            any_space, pl.BlockSpec(memory_space=pltpu.SMEM), any_space, any_space,
            pl.BlockSpec(memory_space=pltpu.VMEM),
        ],
        out_specs=any_space,
        scratch_shapes=[
            *[pltpu.VMEM((2 * part_dev, fields, layers, 8, lon), f32) for _ in range(chunks)],
            pltpu.VMEM((part_dev, fields, layers, padded, wide), f32),
            pltpu.VMEM((part_dev, layers, padded + 8, wide), f32),
            pltpu.VMEM((layers, padded, wide), f32),
            pltpu.VMEM((part_dev, SUBSTEPS, layers, padded, wide), f32),
            pltpu.VMEM(forcing.shape, forcing.dtype),
            pltpu.VMEM(depth.shape, f32),
            pltpu.VMEM((2, part_dev, fields, layers, 8, lon), f32),
            dma((2 * chunks,)), dma((2 * chunks,)), dma((chunks,)), dma((2,)), dma((6,)), dma((6,)), dma((2,)),
        ],
        compiler_params=pltpu.CompilerParams(
            collective_id=0, has_side_effects=True, vmem_limit_bytes=60 * 2**20
        ),
        name="forecast",
    )(ensemble, ancestors, depth, forcing, turn)
    block = pl.BlockSpec((1, 1, layers, rows, lon), lambda p, f: (p, f, 0, 0, 0))
    return pl.pallas_call(
        hand_over,
        out_shape=jax.ShapeDtypeStruct(ensemble.shape, f32),
        grid=(part_dev, fields),
        in_specs=[block],
        out_specs=block,
        name="hand_over",
    )(result)


def solution(mesh):
    in_specs = (
        P("ens", None, None, "lat", None),
        P("ens"),
        P(None, "lat", None),
        P("ens", None, None, "lat", None),
    )
    out_specs = P("ens", None, None, "lat", None)
    return jax.shard_map(
        functools.partial(on_device, mesh.shape["ens"], mesh.shape["lat"]),
        mesh=mesh, in_specs=in_specs, out_specs=out_specs, check_vma=False,
    )
```
